32 devices in a mesh: gx: 8 (over y, x, core), gy: 4 (over z).
Axes of the slice: x: 2, y: 2, z: 4, core: 2. Of those that a mesh axis runs over, the one named last changes fastest.
Arguments:
- test_block: float32 [32, 8, 128, 512], P(None, None, 'gx', 'gy'), may hold values from -1500 to 1500, as said below
- kappa_sq: float32 [8, 128, 512], P(None, 'gx', 'gy'), may hold values from 0.05 to 2
Outputs:
- basis: float32 [32, 8, 128, 512], P(None, None, 'gx', 'gy')
The draws below stay inside these ranges and needn't reach their ends.
Inputs may be any that keep to these rules, and one draw needn't show every extreme that they name: `test_block`: real-valued entries.
All inputs are finite; a program needn't handle non-finite values.
Results may differ from the reference program's by a relative error of at most 0.0003.
Values sent between devices are 32-bit elements; how exact they have to be, the bound alone decides.
A program may use at most 64 MiB of HBM per device.

```python
import math
import jax
import jax.numpy as jnp
from jax import lax

COLS = 32
NZ = 8
NX = 128
NY = 512
CELLS = 524288


def draw_test_block(key, part):
    key_own = jax.random.fold_in(key, 11)
    key_shared = jax.random.fold_in(key, 23)
    key_scale = jax.random.fold_in(key, 37)
    key_weights = jax.random.fold_in(key, 41)
    x_pos = jnp.arange(NX, dtype=jnp.float32) / NX
    y_pos = jnp.arange(NY, dtype=jnp.float32) / NY
    x_upper = (jnp.arange(NX, dtype=jnp.int32) >= NX // 2)[:, None]
    y_upper = (jnp.arange(NY, dtype=jnp.int32) >= NY // 2)[None, :]
    weights = jnp.clip(jax.random.normal(key_weights, (4, COLS), jnp.float32), -2.5, 2.5)
    first = weights[0][:, None, None, None]
    second = weights[1][:, None, None, None]
    third = weights[2][:, None, None, None]
    fourth = weights[3][:, None, None, None]
    region_weight = jnp.where(x_upper, jnp.where(y_upper, fourth, third), jnp.where(y_upper, second, first))
    cell_scale = jnp.exp(jax.random.uniform(key_scale, (1, NZ, NX, NY), jnp.float32) * math.log(10.0))
    own = jnp.clip(jax.random.normal(key_own, (COLS, NZ, NX, NY), jnp.float32), -6.0, 6.0)
    shared = jnp.clip(jax.random.normal(key_shared, (1, NZ, NX, NY), jnp.float32), -6.0, 6.0)
    mixing = 130.0
    trend = (1.0 + 2.0 * x_pos)[:, None] * (1.0 + 2.0 * y_pos)[None, :]
    return cell_scale * trend * (shared * region_weight + own / mixing)


def shard_levels(own_key, dims, shards, low, top_value):
    level, own = 1.0, jax.random.fold_in(own_key, 6)
    for axis_at, shards_of in shards:
        steps = jnp.exp(jax.random.uniform(jax.random.fold_in(own, axis_at), (shards_of,), jnp.float32, low / len(shards), top_value / len(shards)))
        level = level * jnp.repeat(steps, dims[axis_at] // shards_of).reshape([-1 if axis == axis_at else 1 for axis in range(len(dims))])
    return level


def setup_inputs(seed: int = 0) -> dict:
    arg_keys = jax.random.split(jax.random.key(seed), 3)
    return {
        "test_block": draw_test_block(jax.random.fold_in(arg_keys[2], 71), 0),
        "kappa_sq": jnp.clip(jnp.exp(math.log(2.0) - 3.6888794 * jax.random.uniform(arg_keys[1], (NZ, NX, NY), jnp.float32) ** shard_levels(arg_keys[1], (NZ, NX, NY), ((1, 8), (2, 4)), -0.2, 0.2)), 0.05, 2.0),
    }


def stencil(field_in, coefficient):
    padded = jnp.pad(field_in, 1)
    neighbours = padded[1:-1, 2:, 1:-1] + padded[1:-1, :-2, 1:-1]
    neighbours = neighbours + padded[1:-1, 1:-1, 2:] + padded[1:-1, 1:-1, :-2]
    neighbours = neighbours + padded[2:, 1:-1, 1:-1] + padded[:-2, 1:-1, 1:-1]
    return (6.0 + coefficient) * field_in - neighbours

def lower_solve(factor, block):
    return lax.linalg.triangular_solve(factor, block, left_side=True, lower=True)

def reference(test_block, kappa_sq):

    def twice_applied(column):
        return stencil(stencil(column, kappa_sq), kappa_sq)
    sample = lax.map(twice_applied, test_block)
    flattened = sample.reshape(COLS, -1)
    gram_one = jnp.dot(flattened, flattened.T, precision=lax.Precision.HIGHEST)
    factor_one = jnp.linalg.cholesky(gram_one)
    levels = jnp.arange(NZ, dtype=jnp.int32)

    def slab_gram(level):
        slab_block = lax.dynamic_index_in_dim(sample, level, 1, keepdims=False).reshape(COLS, -1)
        partial_value = lower_solve(factor_one, slab_block)
        return jnp.dot(partial_value, partial_value.T, precision=lax.Precision.HIGHEST)
    gram_two = lax.optimization_barrier(jnp.sum(lax.map(slab_gram, levels), axis=0))
    factor_two = jnp.linalg.cholesky(gram_two)
    scale_factor = math.sqrt(CELLS)

    def slab_basis(level):
        slab_block = lax.dynamic_index_in_dim(sample, level, 1, keepdims=False).reshape(COLS, -1)
        partial_value = lower_solve(factor_one, slab_block)
        return lower_solve(factor_two, partial_value) * scale_factor
    stacked = lax.map(slab_basis, levels)
    return stacked.reshape(NZ, COLS, NX, NY).transpose(1, 0, 2, 3)
```

```python
import functools
import math

import jax
import jax.numpy as jnp
from jax import lax
from jax.experimental import pallas as pl
from jax.experimental.pallas import tpu as pltpu
from jax.sharding import PartitionSpec as P

F32 = jnp.float32
BF16 = jnp.bfloat16
LANES = 128


def split(value, terms):
    pieces = []
    for _ in range(terms):
        piece = value.astype(BF16)
        pieces.append(piece)
        value = value - piece.astype(F32)
    return pieces


def fold_rows(block, cols, terms):
    total = block[:cols]
    for i in range(1, terms):
        total = total + block[i * cols:(i + 1) * cols]
    return total


def inverse_factor(gram, cols):
    rows = lax.broadcasted_iota(jnp.int32, (cols, 2 * cols), 0)
    lanes = lax.broadcasted_iota(jnp.int32, (cols, 2 * cols), 1)
    identity = jnp.where(rows + cols == lanes, 1.0, 0.0).astype(F32)
    work = jnp.concatenate([gram, identity[:, cols:]], axis=1)
    pivots = jnp.zeros((cols, 2 * cols), F32)
    for j in range(cols):
        column = jnp.broadcast_to(work[:, j:j + 1], (cols, 2 * cols))
        pivot = column[j:j + 1]
        scaled = work[j:j + 1] * (1.0 / pivot)
        pivots = jnp.where(rows == j, column, pivots)
        work = jnp.where(rows > j, work - column * scaled, work)
    return work[:, cols:] * lax.rsqrt(pivots[:, cols:])


def kernel(sizes, x_ref, kappa_ref, o_ref, first, second, parts, halves, packed, landed, gather_x, gather_y,
           face_send, face_recv, gx_send, gx_recv, gy_send, gy_recv):
    n_gx, n_gy, cols, nz, nx = sizes
    me_x, me_y = lax.axis_index("gx"), lax.axis_index("gy")
    groups = nz * nx
    lane = lax.broadcasted_iota(jnp.int32, (cols, LANES), 1)

    barrier = pltpu.get_barrier_semaphore()

    def at_x(index):
        return {"gx": index, "gy": me_y}

    def at_y(index):
        return {"gx": me_x, "gy": index}

    @pl.loop(1, n_gx)
    def _(k):
        pl.semaphore_signal(barrier, inc=1, device_id=at_x(lax.rem(me_x + k, n_gx)))

    @pl.loop(1, n_gy)
    def _(k):
        pl.semaphore_signal(barrier, inc=1, device_id=at_y(lax.rem(me_y + k, n_gy)))

    def pack(x, values, state):
        low, high = state
        for z in range(nz):
            g = z * nx + x
            rolled = pltpu.roll(values[z], g, 1)
            low = jnp.where(lane == g, rolled, low)
            high = jnp.where(lane == lax.rem(g + LANES - 1, LANES), rolled, high)
        return low, high

    def take(x, state):
        values = []
        for z in range(nz):
            value = x_ref[pl.ds(z * nx + x, cols, stride=groups), :]
            first[z, x + 1] = value
            values.append(value)
        return pack(x, values, state)

    def copies(field, phase):
        up_x = pltpu.make_async_remote_copy(
            src_ref=field.at[:, nx], dst_ref=field.at[:, 0], send_sem=face_send.at[phase, 0],
            recv_sem=face_recv.at[phase, 0], device_id=at_x(me_x + 1))
        down_x = pltpu.make_async_remote_copy(
            src_ref=field.at[:, 1], dst_ref=field.at[:, nx + 1], send_sem=face_send.at[phase, 1],
            recv_sem=face_recv.at[phase, 1], device_id=at_x(me_x - 1))
        up_y = pltpu.make_async_remote_copy(
            src_ref=packed.at[phase, 1], dst_ref=landed.at[phase, 0], send_sem=face_send.at[phase, 2],
            recv_sem=face_recv.at[phase, 2], device_id=at_y(me_y + 1))
        down_y = pltpu.make_async_remote_copy(
            src_ref=packed.at[phase, 0], dst_ref=landed.at[phase, 1], send_sem=face_send.at[phase, 3],
            recv_sem=face_recv.at[phase, 3], device_id=at_y(me_y - 1))
        return up_x, down_x, up_y, down_y

    def send(up, down, index, count):
        @pl.when(index < count - 1)
        def _():
            up.start()

        @pl.when(index > 0)
        def _():
            down.start()

    def receive(up, down, index, count):
        @pl.when(index > 0)
        def _():
            up.wait_recv()

        @pl.when(index < count - 1)
        def _():
            down.wait_recv()

    def finish(up, down, index, count):
        @pl.when(index < count - 1)
        def _():
            up.wait_send()

        @pl.when(index > 0)
        def _():
            down.wait_send()

    for field in (first, second):
        @pl.when(me_x == 0)
        def _():
            field[:, 0] = jnp.zeros((nz, cols, LANES), F32)

        @pl.when(me_x == n_gx - 1)
        def _():
            field[:, nx + 1] = jnp.zeros((nz, cols, LANES), F32)

    for phase in range(2):
        @pl.when(me_y == 0)
        def _():
            landed[phase, 0] = jnp.zeros((cols, LANES), F32)

        @pl.when(me_y == n_gy - 1)
        def _():
            landed[phase, 1] = jnp.zeros((cols, LANES), F32)

    zero = jnp.zeros((cols, LANES), F32)
    state = lax.fori_loop(0, 2, lambda i, s: take(i * (nx - 1), s), (zero, zero))
    pl.semaphore_wait(barrier, n_gx + n_gy - 2)
    up_x, down_x, up_y, down_y = copies(first, 0)
    send(up_x, down_x, me_x, n_gx)
    state = lax.fori_loop(1, nx - 1, take, state)
    packed[0, 0], packed[0, 1] = state
    send(up_y, down_y, me_y, n_gy)

    def apply_plane(field, phase, x):
        from_low, from_high = landed[phase, 0], landed[phase, 1]
        results = []
        for z in range(nz):
            g = z * nx + x
            center = field[z, x + 1]
            halo = jnp.where(lane == lax.rem(g + LANES - 1, LANES), from_low, from_high)
            halo = pltpu.roll(halo, lax.rem(LANES - g, LANES), 1)
            below = pltpu.roll(jnp.where(lane == LANES - 1, halo, center), 1, 1)
            above = pltpu.roll(jnp.where(lane == 0, halo, center), LANES - 1, 1)
            neighbours = field[z, x] + field[z, x + 2]
            neighbours = neighbours + (below + above)
            if z > 0:
                neighbours = neighbours + field[z - 1, x + 1]
            if z < nz - 1:
                neighbours = neighbours + field[z + 1, x + 1]
            coefficient = 6.0 + kappa_ref[pl.ds(g, 1), :]
            results.append(coefficient * center - neighbours)
        return results

    def first_plane(x, state):
        values = apply_plane(first, 0, x)
        for z in range(nz):
            second[z, x + 1] = values[z]
        return pack(x, values, state)

    receive(up_y, down_y, me_y, n_gy)
    state = lax.fori_loop(1, nx - 1, first_plane, (zero, zero))
    receive(up_x, down_x, me_x, n_gx)
    state = lax.fori_loop(0, 2, lambda i, s: first_plane(i * (nx - 1), s), state)
    packed[1, 0], packed[1, 1] = state
    finish(up_x, down_x, me_x, n_gx)
    finish(up_y, down_y, me_y, n_gy)
    up_x, down_x, up_y, down_y = copies(second, 1)
    send(up_y, down_y, me_y, n_gy)
    send(up_x, down_x, me_x, n_gx)

    def square(block):
        return lax.dot_general(block, block, (((1,), (1,)), ((), ())), preferred_element_type=F32)

    def second_plane(x, gram):
        values = apply_plane(second, 1, x)
        for pair in range(nz // 2):
            both = jnp.concatenate(values[2 * pair:2 * pair + 2], axis=1)
            block = jnp.concatenate(split(both, 3), axis=0)
            parts[x, pair] = block
            gram = gram + square(block)
        return gram

    receive(up_y, down_y, me_y, n_gy)
    gram = lax.fori_loop(1, nx - 1, second_plane, jnp.zeros((3 * cols, 3 * cols), F32))
    receive(up_x, down_x, me_x, n_gx)
    gram = lax.fori_loop(0, 2, lambda i, s: second_plane(i * (nx - 1), s), gram)
    finish(up_x, down_x, me_x, n_gx)
    finish(up_y, down_y, me_y, n_gy)

    def fold(gram, terms):
        rows = fold_rows(gram, cols, terms)
        total = rows[:, :cols]
        for i in range(1, terms):
            total = total + rows[:, i * cols:(i + 1) * cols]
        return total

    def exchange(slots, stage, value, axis_at, me, count, send_sem, recv_sem):
        slots[stage, me] = value

        def copy(k, slot):
            return pltpu.make_async_remote_copy(
                src_ref=slots.at[stage, slot], dst_ref=slots.at[stage, slot], send_sem=send_sem.at[stage, k],
                recv_sem=recv_sem.at[stage, slot], device_id=axis_at(lax.rem(me + k, count)))

        @pl.loop(1, count)
        def _(k):
            copy(k, me).start()

        @pl.loop(1, count)
        def _(k):
            copy(k, lax.rem(me + k, count)).wait_recv()

        total = slots[stage, 0]
        for i in range(1, count):
            total = total + slots[stage, i]

        @pl.loop(1, count)
        def _(k):
            copy(k, me).wait_send()

        return total

    def reduced(gram, stage):
        per = LANES // cols
        height = cols // per
        dense = jnp.concatenate([gram[i * height:(i + 1) * height] for i in range(per)], axis=1)
        dense = exchange(gather_x, stage, dense, at_x, me_x, n_gx, gx_send, gx_recv)
        dense = exchange(gather_y, stage, dense, at_y, me_y, n_gy, gy_send, gy_recv)
        return jnp.concatenate([dense[:, i * cols:(i + 1) * cols] for i in range(per)], axis=0)

    def stacked(matrix, terms):
        pieces = split(matrix, terms)
        return jnp.concatenate([jnp.concatenate([piece] * terms, axis=1) for piece in pieces], axis=0)

    inverse = stacked(inverse_factor(reduced(fold(gram, 3), 0), cols), 3)

    def solve_plane(x, gram):
        for pair in range(nz // 2):
            product = jnp.dot(inverse, parts[x, pair], preferred_element_type=F32)
            block = jnp.concatenate(split(fold_rows(product, cols, 3), 2), axis=0)
            halves[x, pair] = block
            gram = gram + square(block)
        return gram

    gram = lax.fori_loop(0, nx, solve_plane, jnp.zeros((2 * cols, 2 * cols), F32))
    scale = math.sqrt(n_gx * n_gy * groups * LANES)
    again = stacked(inverse_factor(reduced(fold(gram, 2), 1), cols) * scale, 2)

    @pl.loop(0, nx)
    def _(x):
        for pair in range(nz // 2):
            product = jnp.dot(again, halves[x, pair], preferred_element_type=F32)
            value = fold_rows(product, cols, 2)
            for side in range(2):
                g = (2 * pair + side) * nx + x
                o_ref[pl.ds(g, cols, stride=groups), :] = value[:, side * LANES:(side + 1) * LANES]


def solution(mesh):
    n_gx, n_gy = mesh.shape["gx"], mesh.shape["gy"]

    def body(test_block, kappa_sq):
        cols, nz, nx, ny = test_block.shape
        dma = pltpu.SemaphoreType.DMA
        vmem = pl.BlockSpec(memory_space=pltpu.VMEM)
        height = cols * cols // LANES
        result = pl.pallas_call(
            functools.partial(kernel, (n_gx, n_gy, cols, nz, nx)),
            out_shape=jax.ShapeDtypeStruct((cols * nz * nx, ny), F32),
            in_specs=[vmem, vmem],
            out_specs=vmem,
            scratch_shapes=[
                pltpu.VMEM((nz, nx + 2, cols, ny), F32),
                pltpu.VMEM((nz, nx + 2, cols, ny), F32),
                pltpu.VMEM((nx, nz // 2, 3 * cols, 2 * ny), BF16),
                pltpu.VMEM((nx, nz // 2, 2 * cols, 2 * ny), BF16),
                pltpu.VMEM((2, 2, cols, ny), F32),
                pltpu.VMEM((2, 2, cols, ny), F32),
                pltpu.VMEM((2, n_gx, height, LANES), F32),
                pltpu.VMEM((2, n_gy, height, LANES), F32),
                dma((2, 4)), dma((2, 4)),
                dma((2, n_gx)), dma((2, n_gx)),
                dma((2, n_gy)), dma((2, n_gy)),
            ],
            compiler_params=pltpu.CompilerParams(
                collective_id=0, has_side_effects=True, vmem_limit_bytes=48 * 1024 * 1024),
        )(test_block.reshape(cols * nz * nx, ny), kappa_sq.reshape(nz * nx, ny))
        return result.reshape(test_block.shape)

    in_specs = (P(None, None, "gx", "gy"), P(None, "gx", "gy"))
    out_specs = P(None, None, "gx", "gy")
    return jax.shard_map(body, mesh=mesh, in_specs=in_specs, out_specs=out_specs, check_vma=False)
```

```python
import functools
import math

import jax
import jax.numpy as jnp
from jax import lax
from jax.experimental import pallas as pl
from jax.experimental.pallas import tpu as pltpu
from jax.sharding import PartitionSpec as P

F32 = jnp.float32
BF16 = jnp.bfloat16
LANES = 128


def split(value, terms):
    pieces = []
    for _ in range(terms):
        piece = value.astype(BF16)
        pieces.append(piece)
        value = value - piece.astype(F32)
    return pieces


def fold_rows(block, cols, terms):
    total = block[:cols]
    for i in range(1, terms):
        total = total + block[i * cols:(i + 1) * cols]
    return total


def inverse_factor(gram, cols):
    rows = lax.broadcasted_iota(jnp.int32, (cols, 2 * cols), 0)
    lanes = lax.broadcasted_iota(jnp.int32, (cols, 2 * cols), 1)
    identity = jnp.where(rows + cols == lanes, 1.0, 0.0).astype(F32)
    work = jnp.concatenate([gram, identity[:, cols:]], axis=1)
    pivots = jnp.zeros((cols, 2 * cols), F32)
    for j in range(cols):
        column = jnp.broadcast_to(work[:, j:j + 1], (cols, 2 * cols))
        pivot = column[j:j + 1]
        scaled = work[j:j + 1] * (1.0 / pivot)
        pivots = jnp.where(rows == j, column, pivots)
        work = jnp.where(rows > j, work - column * scaled, work)
    return work[:, cols:] * lax.rsqrt(pivots[:, cols:])


def kernel(sizes, x_hbm, kappa_hbm, o_ref, x_ref, kappa_ref, load_sem, first, second, parts, halves, packed, landed, gather_x, gather_y,
           face_send, face_recv, gx_send, gx_recv, gy_send, gy_recv):
    n_gx, n_gy, cols, nz, nx = sizes
    me_x, me_y = lax.axis_index("gx"), lax.axis_index("gy")
    groups = nz * nx
    lane = lax.broadcasted_iota(jnp.int32, (cols, LANES), 1)

    load_x = pltpu.make_async_copy(x_hbm, x_ref, load_sem.at[0])
    load_kappa = pltpu.make_async_copy(kappa_hbm, kappa_ref, load_sem.at[1])
    load_x.start()
    load_kappa.start()
    barrier = pltpu.get_barrier_semaphore()

    def at_x(index):
        return {"gx": index, "gy": me_y}

    def at_y(index):
        return {"gx": me_x, "gy": index}

    @pl.loop(1, n_gx)
    def _(k):
        pl.semaphore_signal(barrier, inc=1, device_id=at_x(lax.rem(me_x + k, n_gx)))

    @pl.loop(1, n_gy)
    def _(k):
        pl.semaphore_signal(barrier, inc=1, device_id=at_y(lax.rem(me_y + k, n_gy)))

    def pack(x, values, state):
        low, high = state
        for z in range(nz):
            g = z * nx + x
            rolled = pltpu.roll(values[z], g, 1)
            low = jnp.where(lane == g, rolled, low)
            high = jnp.where(lane == lax.rem(g + LANES - 1, LANES), rolled, high)
        return low, high

    def take(x, state):
        values = []
        for z in range(nz):
            value = x_ref[pl.ds(z * nx + x, cols, stride=groups), :]
            first[z, x + 1] = value
            values.append(value)
        return pack(x, values, state)

    def copies(field, phase):
        up_x = pltpu.make_async_remote_copy(
            src_ref=field.at[:, nx], dst_ref=field.at[:, 0], send_sem=face_send.at[phase, 0],
            recv_sem=face_recv.at[phase, 0], device_id=at_x(me_x + 1))
        down_x = pltpu.make_async_remote_copy(
            src_ref=field.at[:, 1], dst_ref=field.at[:, nx + 1], send_sem=face_send.at[phase, 1],
            recv_sem=face_recv.at[phase, 1], device_id=at_x(me_x - 1))
        return up_x, down_x

    def copies_y(phase, half):
        up_y = pltpu.make_async_remote_copy(
            src_ref=packed.at[phase, half, 1], dst_ref=landed.at[phase, half, 0], device_id=at_y(me_y + 1),
            send_sem=face_send.at[phase, 2 + 2 * half], recv_sem=face_recv.at[phase, 2 + 2 * half])
        down_y = pltpu.make_async_remote_copy(
            src_ref=packed.at[phase, half, 0], dst_ref=landed.at[phase, half, 1], device_id=at_y(me_y - 1),
            send_sem=face_send.at[phase, 3 + 2 * half], recv_sem=face_recv.at[phase, 3 + 2 * half])
        return up_y, down_y

    def send(up, down, index, count):
        @pl.when(index < count - 1)
        def _():
            up.start()

        @pl.when(index > 0)
        def _():
            down.start()

    def receive(up, down, index, count):
        @pl.when(index > 0)
        def _():
            up.wait_recv()

        @pl.when(index < count - 1)
        def _():
            down.wait_recv()

    def finish(up, down, index, count):
        @pl.when(index < count - 1)
        def _():
            up.wait_send()

        @pl.when(index > 0)
        def _():
            down.wait_send()

    for field in (first, second):
        @pl.when(me_x == 0)
        def _():
            field[:, 0] = jnp.zeros((nz, cols, LANES), F32)

        @pl.when(me_x == n_gx - 1)
        def _():
            field[:, nx + 1] = jnp.zeros((nz, cols, LANES), F32)

    for phase in range(2):
        for half in range(2):
            @pl.when(me_y == 0)
            def _():
                landed[phase, half, 0] = jnp.zeros((cols, LANES), F32)

            @pl.when(me_y == n_gy - 1)
            def _():
                landed[phase, half, 1] = jnp.zeros((cols, LANES), F32)

    zero = jnp.zeros((cols, LANES), F32)
    middle = nx // 2
    faces = [copies(first, 0), copies(second, 1)]
    sides = [[copies_y(phase, half) for half in range(2)] for phase in range(2)]

    def edges(step, state):
        return lax.fori_loop(0, 2, lambda i, s: step(i * (nx - 1), s), state)

    def send_side(phase, half, state):
        packed[phase, half, 0], packed[phase, half, 1] = state
        send(*sides[phase][half], me_y, n_gy)

    load_x.wait()
    state = edges(take, (zero, zero))
    pl.semaphore_wait(barrier, n_gx + n_gy - 2)
    send(*faces[0], me_x, n_gx)
    send_side(0, 0, lax.fori_loop(1, middle, take, (zero, zero)))
    send_side(0, 1, lax.fori_loop(middle, nx - 1, take, state))
    load_kappa.wait()

    def apply_plane(field, phase, half, x):
        from_low, from_high = landed[phase, half, 0], landed[phase, half, 1]
        results = []
        for z in range(nz):
            g = z * nx + x
            center = field[z, x + 1]
            halo = jnp.where(lane == lax.rem(g + LANES - 1, LANES), from_low, from_high)
            halo = pltpu.roll(halo, lax.rem(LANES - g, LANES), 1)
            below = pltpu.roll(jnp.where(lane == LANES - 1, halo, center), 1, 1)
            above = pltpu.roll(jnp.where(lane == 0, halo, center), LANES - 1, 1)
            neighbours = field[z, x] + field[z, x + 2]
            neighbours = neighbours + (below + above)
            if z > 0:
                neighbours = neighbours + field[z - 1, x + 1]
            if z < nz - 1:
                neighbours = neighbours + field[z + 1, x + 1]
            coefficient = 6.0 + kappa_ref[pl.ds(g, 1), :]
            results.append(coefficient * center - neighbours)
        return results

    def first_plane(half, x, state):
        values = apply_plane(first, 0, half, x)
        for z in range(nz):
            second[z, x + 1] = values[z]
        return pack(x, values, state)

    receive(*sides[0][0], me_y, n_gy)
    state = lax.fori_loop(1, middle, functools.partial(first_plane, 0), (zero, zero))
    send_side(1, 0, state)
    receive(*sides[0][1], me_y, n_gy)
    receive(*faces[0], me_x, n_gx)
    state = edges(functools.partial(first_plane, 1), (zero, zero))
    send(*faces[1], me_x, n_gx)
    send_side(1, 1, lax.fori_loop(middle, nx - 1, functools.partial(first_plane, 1), state))

    def square(block):
        return lax.dot_general(block, block, (((1,), (1,)), ((), ())), preferred_element_type=F32)

    def second_plane(half, x, gram):
        values = jnp.concatenate(apply_plane(second, 1, half, x), axis=1)
        block = jnp.concatenate(split(values, 3), axis=0)
        parts[x] = block
        return gram + square(block)

    receive(*sides[1][0], me_y, n_gy)
    gram = jnp.zeros((3 * cols, 3 * cols), F32)
    gram = lax.fori_loop(1, middle, functools.partial(second_plane, 0), gram)
    receive(*sides[1][1], me_y, n_gy)
    gram = lax.fori_loop(middle, nx - 1, functools.partial(second_plane, 1), gram)
    receive(*faces[1], me_x, n_gx)
    gram = edges(functools.partial(second_plane, 1), gram)

    def fold(gram, terms):
        rows = fold_rows(gram, cols, terms)
        total = rows[:, :cols]
        for i in range(1, terms):
            total = total + rows[:, i * cols:(i + 1) * cols]
        return total

    def gather_copy(slots, stage, k, slot, axis_at, me, count, send_sem, recv_sem):
        return pltpu.make_async_remote_copy(
            src_ref=slots.at[stage, slot], dst_ref=slots.at[stage, slot], send_sem=send_sem.at[stage, k],
            recv_sem=recv_sem.at[stage, slot], device_id=axis_at(lax.rem(me + k, count)))

    def exchange(slots, stage, value, axis_at, me, count, send_sem, recv_sem):
        slots[stage, me] = value

        def copy(k, slot):
            return gather_copy(slots, stage, k, slot, axis_at, me, count, send_sem, recv_sem)

        @pl.loop(1, count)
        def _(k):
            copy(k, me).start()

        @pl.loop(1, count)
        def _(k):
            copy(k, lax.rem(me + k, count)).wait_recv()

        total = slots[stage, 0]
        for i in range(1, count):
            total = total + slots[stage, i]

        return total

    def reduced(gram, stage):
        per = LANES // cols
        height = cols // per
        dense = jnp.concatenate([gram[i * height:(i + 1) * height] for i in range(per)], axis=1)
        dense = exchange(gather_x, stage, dense, at_x, me_x, n_gx, gx_send, gx_recv)
        dense = exchange(gather_y, stage, dense, at_y, me_y, n_gy, gy_send, gy_recv)
        return jnp.concatenate([dense[:, i * cols:(i + 1) * cols] for i in range(per)], axis=0)

    def rows(stack, order):
        return jnp.concatenate([stack[i * cols:(i + 1) * cols] for i in order], axis=0)

    def columns(matrix, terms, order):
        pieces = split(matrix, terms)
        return jnp.concatenate([pieces[i] for i in order], axis=1)

    inverse = columns(inverse_factor(reduced(fold(gram, 3), 0), cols), 3, (0, 0, 0, 1, 1, 2))

    def solve_plane(x, gram):
        product = jnp.dot(inverse, rows(parts[x], (0, 1, 2, 0, 1, 0)), preferred_element_type=F32)
        block = jnp.concatenate(split(product, 2), axis=0)
        halves[x] = block
        return gram + square(block)

    gram = lax.fori_loop(0, nx, solve_plane, jnp.zeros((2 * cols, 2 * cols), F32), unroll=2)
    scale = math.sqrt(n_gx * n_gy * groups * LANES)
    again = columns(inverse_factor(reduced(fold(gram, 2), 1), cols) * scale, 2, (0, 0, 1, 1))

    def finish_plane(x, carry):
        value = jnp.dot(again, rows(halves[x], (0, 1, 0, 1)), preferred_element_type=F32)
        for z in range(nz):
            o_ref[pl.ds(z * nx + x, cols, stride=groups), :] = value[:, z * LANES:(z + 1) * LANES]
        return carry

    lax.fori_loop(0, nx, finish_plane, 0, unroll=2)

    for phase in range(2):
        finish(*faces[phase], me_x, n_gx)
        for half in range(2):
            finish(*sides[phase][half], me_y, n_gy)
        for slots, axis_at, me, count, send_sem, recv_sem in (
                (gather_x, at_x, me_x, n_gx, gx_send, gx_recv), (gather_y, at_y, me_y, n_gy, gy_send, gy_recv)):
            @pl.loop(1, count)
            def _(k):
                gather_copy(slots, phase, k, me, axis_at, me, count, send_sem, recv_sem).wait_send()


def solution(mesh):
    n_gx, n_gy = mesh.shape["gx"], mesh.shape["gy"]

    def body(test_block, kappa_sq):
        cols, nz, nx, ny = test_block.shape
        dma = pltpu.SemaphoreType.DMA
        vmem = pl.BlockSpec(memory_space=pltpu.VMEM)
        height = cols * cols // LANES
        result = pl.pallas_call(
            functools.partial(kernel, (n_gx, n_gy, cols, nz, nx)),
            out_shape=jax.ShapeDtypeStruct((cols * nz * nx, ny), F32),
            in_specs=[pl.BlockSpec(memory_space=pl.ANY)] * 2,
            out_specs=vmem,
            scratch_shapes=[
                pltpu.VMEM((cols * nz * nx, ny), F32),
                pltpu.VMEM((nz * nx, ny), F32),
                dma((2,)),
                pltpu.VMEM((nz, nx + 2, cols, ny), F32),
                pltpu.VMEM((nz, nx + 2, cols, ny), F32),
                pltpu.VMEM((nx, 3 * cols, nz * ny), BF16),
                pltpu.VMEM((nx, 2 * cols, nz * ny), BF16),
                pltpu.VMEM((2, 2, 2, cols, ny), F32),
                pltpu.VMEM((2, 2, 2, cols, ny), F32),
                pltpu.VMEM((2, n_gx, height, LANES), F32),
                pltpu.VMEM((2, n_gy, height, LANES), F32),
                dma((2, 6)), dma((2, 6)),
                dma((2, n_gx)), dma((2, n_gx)),
                dma((2, n_gy)), dma((2, n_gy)),
            ],
            compiler_params=pltpu.CompilerParams(
                collective_id=0, has_side_effects=True, vmem_limit_bytes=48 * 1024 * 1024),
        )(test_block.reshape(cols * nz * nx, ny), kappa_sq.reshape(nz * nx, ny))
        return result.reshape(test_block.shape)

    in_specs = (P(None, None, "gx", "gy"), P(None, "gx", "gy"))
    out_specs = P(None, None, "gx", "gy")
    return jax.shard_map(body, mesh=mesh, in_specs=in_specs, out_specs=out_specs, check_vma=False)
```

```python
import functools
import math

import jax
import jax.numpy as jnp
from jax import lax
from jax.experimental import pallas as pl
from jax.experimental.pallas import tpu as pltpu
from jax.sharding import PartitionSpec as P

F32 = jnp.float32
BF16 = jnp.bfloat16
LANES = 128


def split(value, terms):
    pieces = []
    for _ in range(terms):
        piece = value.astype(BF16)
        pieces.append(piece)
        value = value - piece.astype(F32)
    return pieces


def fold_rows(block, cols, terms):
    total = block[:cols]
    for i in range(1, terms):
        total = total + block[i * cols:(i + 1) * cols]
    return total


def inverse_factor(gram, cols):
    rows = lax.broadcasted_iota(jnp.int32, (cols, 2 * cols), 0)
    lanes = lax.broadcasted_iota(jnp.int32, (cols, 2 * cols), 1)
    identity = jnp.where(rows + cols == lanes, 1.0, 0.0).astype(F32)
    work = jnp.concatenate([gram, identity[:, cols:]], axis=1)
    pivots = jnp.zeros((cols, 2 * cols), F32)
    for j in range(cols):
        column = jnp.broadcast_to(work[:, j:j + 1], (cols, 2 * cols))
        pivot = column[j:j + 1]
        scaled = work[j:j + 1] * (1.0 / pivot)
        pivots = jnp.where(rows == j, column, pivots)
        work = jnp.where(rows > j, work - column * scaled, work)
    return work[:, cols:] * lax.rsqrt(pivots[:, cols:])


def kernel(sizes, x_hbm, kappa_hbm, o_ref, x_ref, kappa_ref, load_sem, first, second, parts, halves, packed, landed, gather_x, gather_y,
           face_send, face_recv, gx_send, gx_recv, gy_send, gy_recv):
    n_gx, n_gy, cols, nz, nx = sizes
    me_x, me_y = lax.axis_index("gx"), lax.axis_index("gy")
    groups = nz * nx
    lane = lax.broadcasted_iota(jnp.int32, (cols, LANES), 1)

    load_x = pltpu.make_async_copy(x_hbm, x_ref, load_sem.at[0])
    load_kappa = pltpu.make_async_copy(kappa_hbm, kappa_ref, load_sem.at[1])
    load_x.start()
    load_kappa.start()
    barrier = pltpu.get_barrier_semaphore()

    def at_x(index):
        return {"gx": index, "gy": me_y}

    def at_y(index):
        return {"gx": me_x, "gy": index}

    @pl.loop(1, n_gx)
    def _(k):
        pl.semaphore_signal(barrier, inc=1, device_id=at_x(lax.rem(me_x + k, n_gx)))

    @pl.loop(1, n_gy)
    def _(k):
        pl.semaphore_signal(barrier, inc=1, device_id=at_y(lax.rem(me_y + k, n_gy)))

    def pack(x, values, state):
        low, high = state
        for z in range(nz):
            g = z * nx + x
            rolled = pltpu.roll(values[z], g, 1)
            low = jnp.where(lane == g, rolled, low)
            high = jnp.where(lane == lax.rem(g + LANES - 1, LANES), rolled, high)
        return low, high

    def take(x, state):
        values = []
        for z in range(nz):
            value = x_ref[pl.ds(z * nx + x, cols, stride=groups), :]
            first[z, x + 1] = value
            values.append(value)
        return pack(x, values, state)

    def copies(field, phase):
        up_x = pltpu.make_async_remote_copy(
            src_ref=field.at[:, nx], dst_ref=field.at[:, 0], send_sem=face_send.at[phase, 0],
            recv_sem=face_recv.at[phase, 0], device_id=at_x(me_x + 1))
        down_x = pltpu.make_async_remote_copy(
            src_ref=field.at[:, 1], dst_ref=field.at[:, nx + 1], send_sem=face_send.at[phase, 1],
            recv_sem=face_recv.at[phase, 1], device_id=at_x(me_x - 1))
        return up_x, down_x

    def copies_y(phase, half):
        up_y = pltpu.make_async_remote_copy(
            src_ref=packed.at[phase, half, 1], dst_ref=landed.at[phase, half, 0], device_id=at_y(me_y + 1),
            send_sem=face_send.at[phase, 2 + 2 * half], recv_sem=face_recv.at[phase, 2 + 2 * half])
        down_y = pltpu.make_async_remote_copy(
            src_ref=packed.at[phase, half, 0], dst_ref=landed.at[phase, half, 1], device_id=at_y(me_y - 1),
            send_sem=face_send.at[phase, 3 + 2 * half], recv_sem=face_recv.at[phase, 3 + 2 * half])
        return up_y, down_y

    def send(up, down, index, count):
        @pl.when(index < count - 1)
        def _():
            up.start()

        @pl.when(index > 0)
        def _():
            down.start()

    def receive(up, down, index, count):
        @pl.when(index > 0)
        def _():
            up.wait_recv()

        @pl.when(index < count - 1)
        def _():
            down.wait_recv()

    def finish(up, down, index, count):
        @pl.when(index < count - 1)
        def _():
            up.wait_send()

        @pl.when(index > 0)
        def _():
            down.wait_send()

    for field in (first, second):
        @pl.when(me_x == 0)
        def _():
            field[:, 0] = jnp.zeros((nz, cols, LANES), F32)

        @pl.when(me_x == n_gx - 1)
        def _():
            field[:, nx + 1] = jnp.zeros((nz, cols, LANES), F32)

    for phase in range(2):
        for half in range(2):
            @pl.when(me_y == 0)
            def _():
                landed[phase, half, 0] = jnp.zeros((cols, LANES), F32)

            @pl.when(me_y == n_gy - 1)
            def _():
                landed[phase, half, 1] = jnp.zeros((cols, LANES), F32)

    zero = jnp.zeros((cols, LANES), F32)
    middle = nx // 2
    faces = [copies(first, 0), copies(second, 1)]
    sides = [[copies_y(phase, half) for half in range(2)] for phase in range(2)]

    def edges(step, state):
        return lax.fori_loop(0, 2, lambda i, s: step(i * (nx - 1), s), state)

    def send_side(phase, half, state):
        packed[phase, half, 0], packed[phase, half, 1] = state
        send(*sides[phase][half], me_y, n_gy)

    load_x.wait()
    state = edges(take, (zero, zero))
    pl.semaphore_wait(barrier, n_gx + n_gy - 2)
    send(*faces[0], me_x, n_gx)
    send_side(0, 0, lax.fori_loop(1, middle, take, (zero, zero)))
    send_side(0, 1, lax.fori_loop(middle, nx - 1, take, state))
    load_kappa.wait()

    def apply_plane(field, phase, half, x):
        from_low, from_high = landed[phase, half, 0], landed[phase, half, 1]
        results = []
        for z in range(nz):
            g = z * nx + x
            center = field[z, x + 1]
            halo = jnp.where(lane == lax.rem(g + LANES - 1, LANES), from_low, from_high)
            halo = pltpu.roll(halo, lax.rem(LANES - g, LANES), 1)
            below = pltpu.roll(jnp.where(lane == LANES - 1, halo, center), 1, 1)
            above = pltpu.roll(jnp.where(lane == 0, halo, center), LANES - 1, 1)
            neighbours = field[z, x] + field[z, x + 2]
            neighbours = neighbours + (below + above)
            if z > 0:
                neighbours = neighbours + field[z - 1, x + 1]
            if z < nz - 1:
                neighbours = neighbours + field[z + 1, x + 1]
            coefficient = 6.0 + kappa_ref[pl.ds(g, 1), :]
            results.append(coefficient * center - neighbours)
        return results

    def first_plane(half, x, state):
        values = apply_plane(first, 0, half, x)
        for z in range(nz):
            second[z, x + 1] = values[z]
        return pack(x, values, state)

    receive(*sides[0][0], me_y, n_gy)
    state = lax.fori_loop(1, middle, functools.partial(first_plane, 0), (zero, zero))
    send_side(1, 0, state)
    receive(*sides[0][1], me_y, n_gy)
    receive(*faces[0], me_x, n_gx)
    state = edges(functools.partial(first_plane, 1), (zero, zero))
    send(*faces[1], me_x, n_gx)
    send_side(1, 1, lax.fori_loop(middle, nx - 1, functools.partial(first_plane, 1), state))

    def square(block):
        return lax.dot_general(block, block, (((1,), (1,)), ((), ())), preferred_element_type=F32)

    def second_plane(half, x, gram):
        values = jnp.concatenate(apply_plane(second, 1, half, x), axis=1)
        block = jnp.concatenate(split(values, 3), axis=0)
        parts[x] = block
        return gram + square(block)

    receive(*sides[1][0], me_y, n_gy)
    gram = jnp.zeros((3 * cols, 3 * cols), F32)
    gram = lax.fori_loop(1, middle, functools.partial(second_plane, 0), gram, unroll=True)
    receive(*sides[1][1], me_y, n_gy)
    gram = lax.fori_loop(middle, nx - 1, functools.partial(second_plane, 1), gram, unroll=True)
    receive(*faces[1], me_x, n_gx)
    gram = edges(functools.partial(second_plane, 1), gram)

    def fold(gram, terms):
        rows = fold_rows(gram, cols, terms)
        total = rows[:, :cols]
        for i in range(1, terms):
            total = total + rows[:, i * cols:(i + 1) * cols]
        return total

    def gather_copy(slots, stage, k, slot, axis_at, me, count, send_sem, recv_sem):
        return pltpu.make_async_remote_copy(
            src_ref=slots.at[stage, slot], dst_ref=slots.at[stage, slot], send_sem=send_sem.at[stage, k],
            recv_sem=recv_sem.at[stage, slot], device_id=axis_at(lax.rem(me + k, count)))

    def exchange(slots, stage, value, axis_at, me, count, send_sem, recv_sem):
        slots[stage, me] = value

        def copy(k, slot):
            return gather_copy(slots, stage, k, slot, axis_at, me, count, send_sem, recv_sem)

        @pl.loop(1, count)
        def _(k):
            copy(k, me).start()

        @pl.loop(1, count)
        def _(k):
            copy(k, lax.rem(me + k, count)).wait_recv()

        total = slots[stage, 0]
        for i in range(1, count):
            total = total + slots[stage, i]

        return total

    def reduced(gram, stage):
        per = LANES // cols
        height = cols // per
        dense = jnp.concatenate([gram[i * height:(i + 1) * height] for i in range(per)], axis=1)
        dense = exchange(gather_x, stage, dense, at_x, me_x, n_gx, gx_send, gx_recv)
        dense = exchange(gather_y, stage, dense, at_y, me_y, n_gy, gy_send, gy_recv)
        return jnp.concatenate([dense[:, i * cols:(i + 1) * cols] for i in range(per)], axis=0)

    def rows(stack, order):
        return jnp.concatenate([stack[i * cols:(i + 1) * cols] for i in order], axis=0)

    def columns(matrix, terms, order):
        pieces = split(matrix, terms)
        return jnp.concatenate([pieces[i] for i in order], axis=1)

    inverse = columns(inverse_factor(reduced(fold(gram, 3), 0), cols), 3, (0, 0, 0, 1, 1, 2))

    def solve_plane(x, gram):
        product = jnp.dot(inverse, rows(parts[x], (0, 1, 2, 0, 1, 0)), preferred_element_type=F32)
        block = jnp.concatenate(split(product, 2), axis=0)
        halves[x] = block
        return gram + square(block)

    gram = lax.fori_loop(0, nx, solve_plane, jnp.zeros((2 * cols, 2 * cols), F32), unroll=4)
    scale = math.sqrt(n_gx * n_gy * groups * LANES)
    again = columns(inverse_factor(reduced(fold(gram, 2), 1), cols) * scale, 2, (0, 0, 1, 1))

    def finish_plane(x, carry):
        value = jnp.dot(again, rows(halves[x], (0, 1, 0, 1)), preferred_element_type=F32)
        for z in range(nz):
            o_ref[pl.ds(z * nx + x, cols, stride=groups), :] = value[:, z * LANES:(z + 1) * LANES]
        return carry

    lax.fori_loop(0, nx, finish_plane, 0, unroll=4)

    for phase in range(2):
        finish(*faces[phase], me_x, n_gx)
        for half in range(2):
            finish(*sides[phase][half], me_y, n_gy)
        for slots, axis_at, me, count, send_sem, recv_sem in (
                (gather_x, at_x, me_x, n_gx, gx_send, gx_recv), (gather_y, at_y, me_y, n_gy, gy_send, gy_recv)):
            @pl.loop(1, count)
            def _(k):
                gather_copy(slots, phase, k, me, axis_at, me, count, send_sem, recv_sem).wait_send()


def solution(mesh):
    n_gx, n_gy = mesh.shape["gx"], mesh.shape["gy"]

    def body(test_block, kappa_sq):
        cols, nz, nx, ny = test_block.shape
        dma = pltpu.SemaphoreType.DMA
        vmem = pl.BlockSpec(memory_space=pltpu.VMEM)
        height = cols * cols // LANES
        result = pl.pallas_call(
            functools.partial(kernel, (n_gx, n_gy, cols, nz, nx)),
            out_shape=jax.ShapeDtypeStruct((cols * nz * nx, ny), F32),
            in_specs=[pl.BlockSpec(memory_space=pltpu.HBM)] * 2,
            out_specs=vmem,
            scratch_shapes=[
                pltpu.VMEM((cols * nz * nx, ny), F32),
                pltpu.VMEM((nz * nx, ny), F32),
                dma((2,)),
                pltpu.VMEM((nz, nx + 2, cols, ny), F32),
                pltpu.VMEM((nz, nx + 2, cols, ny), F32),
                pltpu.VMEM((nx, 3 * cols, nz * ny), BF16),
                pltpu.VMEM((nx, 2 * cols, nz * ny), BF16),
                pltpu.VMEM((2, 2, 2, cols, ny), F32),
                pltpu.VMEM((2, 2, 2, cols, ny), F32),
                pltpu.VMEM((2, n_gx, height, LANES), F32),
                pltpu.VMEM((2, n_gy, height, LANES), F32),
                dma((2, 6)), dma((2, 6)),
                dma((2, n_gx)), dma((2, n_gx)),
                dma((2, n_gy)), dma((2, n_gy)),
            ],
            compiler_params=pltpu.CompilerParams(
                collective_id=0, has_side_effects=True, vmem_limit_bytes=48 * 1024 * 1024),
        )(test_block.reshape(cols * nz * nx, ny), kappa_sq.reshape(nz * nx, ny))
        return result.reshape(test_block.shape)

    in_specs = (P(None, None, "gx", "gy"), P(None, "gx", "gy"))
    out_specs = P(None, None, "gx", "gy")
    return jax.shard_map(body, mesh=mesh, in_specs=in_specs, out_specs=out_specs, check_vma=False)
```

```python
import functools
import math

import jax
import jax.numpy as jnp
from jax import lax
from jax.experimental import pallas as pl
from jax.experimental.pallas import tpu as pltpu
from jax.sharding import PartitionSpec as P

F32 = jnp.float32
BF16 = jnp.bfloat16
LANES = 128


def split(value, terms):
    pieces = []
    for _ in range(terms):
        piece = value.astype(BF16)
        pieces.append(piece)
        value = value - piece.astype(F32)
    return pieces


def fold_rows(block, cols, terms):
    total = block[:cols]
    for i in range(1, terms):
        total = total + block[i * cols:(i + 1) * cols]
    return total


def inverse_factor(gram, cols):
    rows = lax.broadcasted_iota(jnp.int32, (cols, 2 * cols), 0)
    lanes = lax.broadcasted_iota(jnp.int32, (cols, 2 * cols), 1)
    identity = jnp.where(rows + cols == lanes, 1.0, 0.0).astype(F32)
    work = jnp.concatenate([gram, identity[:, cols:]], axis=1)
    pivots = jnp.zeros((cols, 2 * cols), F32)
    for j in range(cols):
        column = jnp.broadcast_to(work[:, j:j + 1], (cols, 2 * cols))
        pivot = column[j:j + 1]
        scaled = work[j:j + 1] * (1.0 / pivot)
        pivots = jnp.where(rows == j, column, pivots)
        work = jnp.where(rows > j, work - column * scaled, work)
    return work[:, cols:] * lax.rsqrt(pivots[:, cols:])


def kernel(sizes, x_hbm, kappa_hbm, halves_hbm, again_ref, x_ref, kappa_ref, load_sem, store_sem, first, second, parts, halves, packed, landed, gather_x, gather_y,
           face_send, face_recv, gx_send, gx_recv, gy_send, gy_recv):
    n_gx, n_gy, cols, nz, nx = sizes
    me_x, me_y = lax.axis_index("gx"), lax.axis_index("gy")
    groups = nz * nx
    lane = lax.broadcasted_iota(jnp.int32, (cols, LANES), 1)

    load_x = pltpu.make_async_copy(x_hbm, x_ref, load_sem.at[0])
    load_kappa = pltpu.make_async_copy(kappa_hbm, kappa_ref, load_sem.at[1])
    load_x.start()
    load_kappa.start()
    barrier = pltpu.get_barrier_semaphore()

    def at_x(index):
        return {"gx": index, "gy": me_y}

    def at_y(index):
        return {"gx": me_x, "gy": index}

    @pl.loop(1, n_gx)
    def _(k):
        pl.semaphore_signal(barrier, inc=1, device_id=at_x(lax.rem(me_x + k, n_gx)))

    @pl.loop(1, n_gy)
    def _(k):
        pl.semaphore_signal(barrier, inc=1, device_id=at_y(lax.rem(me_y + k, n_gy)))

    def pack(x, values, state):
        low, high = state
        for z in range(nz):
            g = z * nx + x
            rolled = pltpu.roll(values[z], g, 1)
            low = jnp.where(lane == g, rolled, low)
            high = jnp.where(lane == lax.rem(g + LANES - 1, LANES), rolled, high)
        return low, high

    def take(x, state):
        values = []
        for z in range(nz):
            value = x_ref[pl.ds(z * nx + x, cols, stride=groups), :]
            first[z, x + 1] = value
            values.append(value)
        return pack(x, values, state)

    def copies(field, phase):
        up_x = pltpu.make_async_remote_copy(
            src_ref=field.at[:, nx], dst_ref=field.at[:, 0], send_sem=face_send.at[phase, 0],
            recv_sem=face_recv.at[phase, 0], device_id=at_x(me_x + 1))
        down_x = pltpu.make_async_remote_copy(
            src_ref=field.at[:, 1], dst_ref=field.at[:, nx + 1], send_sem=face_send.at[phase, 1],
            recv_sem=face_recv.at[phase, 1], device_id=at_x(me_x - 1))
        return up_x, down_x

    def copies_y(phase, half):
        up_y = pltpu.make_async_remote_copy(
            src_ref=packed.at[phase, half, 1], dst_ref=landed.at[phase, half, 0], device_id=at_y(me_y + 1),
            send_sem=face_send.at[phase, 2 + 2 * half], recv_sem=face_recv.at[phase, 2 + 2 * half])
        down_y = pltpu.make_async_remote_copy(
            src_ref=packed.at[phase, half, 0], dst_ref=landed.at[phase, half, 1], device_id=at_y(me_y - 1),
            send_sem=face_send.at[phase, 3 + 2 * half], recv_sem=face_recv.at[phase, 3 + 2 * half])
        return up_y, down_y

    def send(up, down, index, count):
        @pl.when(index < count - 1)
        def _():
            up.start()

        @pl.when(index > 0)
        def _():
            down.start()

    def receive(up, down, index, count):
        @pl.when(index > 0)
        def _():
            up.wait_recv()

        @pl.when(index < count - 1)
        def _():
            down.wait_recv()

    def finish(up, down, index, count):
        @pl.when(index < count - 1)
        def _():
            up.wait_send()

        @pl.when(index > 0)
        def _():
            down.wait_send()

    for field in (first, second):
        @pl.when(me_x == 0)
        def _():
            field[:, 0] = jnp.zeros((nz, cols, LANES), F32)

        @pl.when(me_x == n_gx - 1)
        def _():
            field[:, nx + 1] = jnp.zeros((nz, cols, LANES), F32)

    for phase in range(2):
        for half in range(2):
            @pl.when(me_y == 0)
            def _():
                landed[phase, half, 0] = jnp.zeros((cols, LANES), F32)

            @pl.when(me_y == n_gy - 1)
            def _():
                landed[phase, half, 1] = jnp.zeros((cols, LANES), F32)

    zero = jnp.zeros((cols, LANES), F32)
    middle = nx // 2
    faces = [copies(first, 0), copies(second, 1)]
    sides = [[copies_y(phase, half) for half in range(2)] for phase in range(2)]

    def edges(step, state):
        return lax.fori_loop(0, 2, lambda i, s: step(i * (nx - 1), s), state)

    def send_side(phase, half, state):
        packed[phase, half, 0], packed[phase, half, 1] = state
        send(*sides[phase][half], me_y, n_gy)

    load_x.wait()
    state = edges(take, (zero, zero))
    pl.semaphore_wait(barrier, n_gx + n_gy - 2)
    send(*faces[0], me_x, n_gx)
    send_side(0, 0, lax.fori_loop(1, middle, take, (zero, zero)))
    send_side(0, 1, lax.fori_loop(middle, nx - 1, take, state))
    load_kappa.wait()

    def apply_plane(field, phase, half, x):
        from_low, from_high = landed[phase, half, 0], landed[phase, half, 1]
        results = []
        for z in range(nz):
            g = z * nx + x
            center = field[z, x + 1]
            halo = jnp.where(lane == lax.rem(g + LANES - 1, LANES), from_low, from_high)
            halo = pltpu.roll(halo, lax.rem(LANES - g, LANES), 1)
            below = pltpu.roll(jnp.where(lane == LANES - 1, halo, center), 1, 1)
            above = pltpu.roll(jnp.where(lane == 0, halo, center), LANES - 1, 1)
            neighbours = field[z, x] + field[z, x + 2]
            neighbours = neighbours + (below + above)
            if z > 0:
                neighbours = neighbours + field[z - 1, x + 1]
            if z < nz - 1:
                neighbours = neighbours + field[z + 1, x + 1]
            coefficient = 6.0 + kappa_ref[pl.ds(g, 1), :]
            results.append(coefficient * center - neighbours)
        return results

    def first_plane(half, x, state):
        values = apply_plane(first, 0, half, x)
        for z in range(nz):
            second[z, x + 1] = values[z]
        return pack(x, values, state)

    receive(*sides[0][0], me_y, n_gy)
    state = lax.fori_loop(1, middle, functools.partial(first_plane, 0), (zero, zero))
    send_side(1, 0, state)
    receive(*sides[0][1], me_y, n_gy)
    receive(*faces[0], me_x, n_gx)
    state = edges(functools.partial(first_plane, 1), (zero, zero))
    send(*faces[1], me_x, n_gx)
    send_side(1, 1, lax.fori_loop(middle, nx - 1, functools.partial(first_plane, 1), state))

    def square(block):
        return lax.dot_general(block, block, (((1,), (1,)), ((), ())), preferred_element_type=F32)

    def second_plane(half, x, gram):
        values = jnp.concatenate(apply_plane(second, 1, half, x), axis=1)
        block = jnp.concatenate(split(values, 3), axis=0)
        parts[x] = block
        return gram + square(block)

    receive(*sides[1][0], me_y, n_gy)
    gram = jnp.zeros((3 * cols, 3 * cols), F32)
    gram = lax.fori_loop(1, middle, functools.partial(second_plane, 0), gram, unroll=True)
    receive(*sides[1][1], me_y, n_gy)
    gram = lax.fori_loop(middle, nx - 1, functools.partial(second_plane, 1), gram, unroll=True)
    receive(*faces[1], me_x, n_gx)
    gram = edges(functools.partial(second_plane, 1), gram)

    def fold(gram, terms):
        rows = fold_rows(gram, cols, terms)
        total = rows[:, :cols]
        for i in range(1, terms):
            total = total + rows[:, i * cols:(i + 1) * cols]
        return total

    def gather_copy(slots, stage, k, slot, axis_at, me, count, send_sem, recv_sem):
        return pltpu.make_async_remote_copy(
            src_ref=slots.at[stage, slot], dst_ref=slots.at[stage, slot], send_sem=send_sem.at[stage, k],
            recv_sem=recv_sem.at[stage, slot], device_id=axis_at(lax.rem(me + k, count)))

    def exchange(slots, stage, value, axis_at, me, count, send_sem, recv_sem):
        slots[stage, me] = value

        def copy(k, slot):
            return gather_copy(slots, stage, k, slot, axis_at, me, count, send_sem, recv_sem)

        @pl.loop(1, count)
        def _(k):
            copy(k, me).start()

        @pl.loop(1, count)
        def _(k):
            copy(k, lax.rem(me + k, count)).wait_recv()

        total = slots[stage, 0]
        for i in range(1, count):
            total = total + slots[stage, i]

        return total

    def reduced(gram, stage):
        per = LANES // cols
        height = cols // per
        dense = jnp.concatenate([gram[i * height:(i + 1) * height] for i in range(per)], axis=1)
        dense = exchange(gather_x, stage, dense, at_x, me_x, n_gx, gx_send, gx_recv)
        dense = exchange(gather_y, stage, dense, at_y, me_y, n_gy, gy_send, gy_recv)
        return jnp.concatenate([dense[:, i * cols:(i + 1) * cols] for i in range(per)], axis=0)

    def rows(stack, order):
        return jnp.concatenate([stack[i * cols:(i + 1) * cols] for i in order], axis=0)

    def columns(matrix, terms, order):
        pieces = split(matrix, terms)
        return jnp.concatenate([pieces[i] for i in order], axis=1)

    inverse = columns(inverse_factor(reduced(fold(gram, 3), 0), cols), 3, (0, 0, 0, 1, 1, 2))

    def solve_plane(x, gram):
        product = jnp.dot(inverse, rows(parts[x], (0, 1, 2, 0, 1, 0)), preferred_element_type=F32)
        block = jnp.concatenate(split(product, 2), axis=0)
        halves[x] = block
        pltpu.make_async_copy(halves.at[x], halves_hbm.at[x], store_sem.at[x]).start()
        return gram + square(block)

    gram = lax.fori_loop(0, nx, solve_plane, jnp.zeros((2 * cols, 2 * cols), F32), unroll=4)
    scale = math.sqrt(n_gx * n_gy * groups * LANES)
    again_ref[...] = columns(inverse_factor(reduced(fold(gram, 2), 1), cols) * scale, 2, (0, 0, 1, 1))

    @pl.loop(0, nx)
    def _(x):
        pltpu.make_async_copy(halves.at[x], halves_hbm.at[x], store_sem.at[x]).wait()

    for phase in range(2):
        finish(*faces[phase], me_x, n_gx)
        for half in range(2):
            finish(*sides[phase][half], me_y, n_gy)
        for slots, axis_at, me, count, send_sem, recv_sem in (
                (gather_x, at_x, me_x, n_gx, gx_send, gx_recv), (gather_y, at_y, me_y, n_gy, gy_send, gy_recv)):
            @pl.loop(1, count)
            def _(k):
                gather_copy(slots, phase, k, me, axis_at, me, count, send_sem, recv_sem).wait_send()


def finish_kernel(again_ref, halves_ref, o_ref):
    cols, deep, nx, ny = o_ref.shape
    flat = o_ref.reshape(cols * deep * nx, ny)

    def plane(x, carry):
        block = halves_ref[x]
        value = jnp.dot(again_ref[...], jnp.concatenate([block, block], axis=0), preferred_element_type=F32)
        for z in range(deep):
            flat[pl.ds(z * nx + x, cols, stride=deep * nx), :] = value[:, z * ny:(z + 1) * ny]
        return carry

    lax.fori_loop(0, nx, plane, 0, unroll=4)


def solution(mesh):
    n_gx, n_gy = mesh.shape["gx"], mesh.shape["gy"]

    def body(test_block, kappa_sq):
        cols, nz, nx, ny = test_block.shape
        dma = pltpu.SemaphoreType.DMA
        vmem = pl.BlockSpec(memory_space=pltpu.VMEM)
        height = cols * cols // LANES
        halves, again = pl.pallas_call(
            functools.partial(kernel, (n_gx, n_gy, cols, nz, nx)),
            out_shape=(jax.ShapeDtypeStruct((nx, 2 * cols, nz * ny), BF16),
                       jax.ShapeDtypeStruct((cols, 4 * cols), BF16)),
            in_specs=[pl.BlockSpec(memory_space=pltpu.HBM)] * 2,
            out_specs=(pl.BlockSpec(memory_space=pltpu.HBM), vmem),
            scratch_shapes=[
                pltpu.VMEM((cols * nz * nx, ny), F32),
                pltpu.VMEM((nz * nx, ny), F32),
                dma((2,)), dma((nx,)),
                pltpu.VMEM((nz, nx + 2, cols, ny), F32),
                pltpu.VMEM((nz, nx + 2, cols, ny), F32),
                pltpu.VMEM((nx, 3 * cols, nz * ny), BF16),
                pltpu.VMEM((nx, 2 * cols, nz * ny), BF16),
                pltpu.VMEM((2, 2, 2, cols, ny), F32),
                pltpu.VMEM((2, 2, 2, cols, ny), F32),
                pltpu.VMEM((2, n_gx, height, LANES), F32),
                pltpu.VMEM((2, n_gy, height, LANES), F32),
                dma((2, 6)), dma((2, 6)),
                dma((2, n_gx)), dma((2, n_gx)),
                dma((2, n_gy)), dma((2, n_gy)),
            ],
            compiler_params=pltpu.CompilerParams(
                collective_id=0, has_side_effects=True, vmem_limit_bytes=62 * 1024 * 1024),
        )(test_block.reshape(cols * nz * nx, ny), kappa_sq.reshape(nz * nx, ny))
        wide = 8
        return pl.pallas_call(
            finish_kernel,
            out_shape=jax.ShapeDtypeStruct(test_block.shape, F32),
            grid=(nx // wide,),
            in_specs=[vmem, pl.BlockSpec((wide, 2 * cols, nz * ny), lambda i: (i, 0, 0))],
            out_specs=pl.BlockSpec((cols, nz, wide, ny), lambda i: (0, 0, i, 0)),
            compiler_params=pltpu.CompilerParams(vmem_limit_bytes=62 * 1024 * 1024),
        )(again, halves)

    in_specs = (P(None, None, "gx", "gy"), P(None, "gx", "gy"))
    out_specs = P(None, None, "gx", "gy")
    return jax.shard_map(body, mesh=mesh, in_specs=in_specs, out_specs=out_specs, check_vma=False)
```

```python
import functools
import math

import jax
import jax.numpy as jnp
from jax import lax
from jax.experimental import pallas as pl
from jax.experimental.pallas import tpu as pltpu
from jax.sharding import PartitionSpec as P

F32 = jnp.float32
BF16 = jnp.bfloat16
LANES = 128


def split(value, terms):
    pieces = []
    for _ in range(terms):
        piece = value.astype(BF16)
        pieces.append(piece)
        value = value - piece.astype(F32)
    return pieces


def fold_rows(block, cols, terms):
    total = block[:cols]
    for i in range(1, terms):
        total = total + block[i * cols:(i + 1) * cols]
    return total


def inverse_factor(gram, cols):
    rows = lax.broadcasted_iota(jnp.int32, (cols, 2 * cols), 0)
    lanes = lax.broadcasted_iota(jnp.int32, (cols, 2 * cols), 1)
    identity = jnp.where(rows + cols == lanes, 1.0, 0.0).astype(F32)
    work = jnp.concatenate([gram, identity[:, cols:]], axis=1)
    pivots = jnp.zeros((cols, 2 * cols), F32)
    for j in range(cols):
        column = jnp.broadcast_to(work[:, j:j + 1], (cols, 2 * cols))
        pivot = column[j:j + 1]
        scaled = work[j:j + 1] * (1.0 / pivot)
        pivots = jnp.where(rows == j, column, pivots)
        work = jnp.where(rows > j, work - column * scaled, work)
    return work[:, cols:] * lax.rsqrt(pivots[:, cols:])


def kernel(sizes, x_hbm, kappa_hbm, halves_hbm, again_ref, x_ref, kappa_ref, load_sem, store_sem, first, second, parts, halves, packed, landed, gather_x, gather_y,
           face_send, face_recv, gx_send, gx_recv, gy_send, gy_recv):
    n_gx, n_gy, cols, nz, nx = sizes
    me_x, me_y = lax.axis_index("gx"), lax.axis_index("gy")
    groups = nz * nx
    lane = lax.broadcasted_iota(jnp.int32, (cols, LANES), 1)

    load_x = pltpu.make_async_copy(x_hbm, x_ref, load_sem.at[0])
    load_kappa = pltpu.make_async_copy(kappa_hbm, kappa_ref, load_sem.at[1])
    load_x.start()
    load_kappa.start()
    barrier = pltpu.get_barrier_semaphore()

    def at_x(index):
        return {"gx": index, "gy": me_y}

    def at_y(index):
        return {"gx": me_x, "gy": index}

    @pl.loop(1, n_gx)
    def _(k):
        pl.semaphore_signal(barrier, inc=1, device_id=at_x(lax.rem(me_x + k, n_gx)))

    @pl.loop(1, n_gy)
    def _(k):
        pl.semaphore_signal(barrier, inc=1, device_id=at_y(lax.rem(me_y + k, n_gy)))

    def pack(x, values, state):
        low, high = state
        for z in range(nz):
            g = z * nx + x
            rolled = pltpu.roll(values[z], g, 1)
            low = jnp.where(lane == g, rolled, low)
            high = jnp.where(lane == lax.rem(g + LANES - 1, LANES), rolled, high)
        return low, high

    def take(x, state):
        values = []
        for z in range(nz):
            value = x_ref[pl.ds(z * nx + x, cols, stride=groups), :]
            first[z, x + 1] = value
            values.append(value)
        return pack(x, values, state)

    def copies(field, phase):
        up_x = pltpu.make_async_remote_copy(
            src_ref=field.at[:, nx], dst_ref=field.at[:, 0], send_sem=face_send.at[phase, 0],
            recv_sem=face_recv.at[phase, 0], device_id=at_x(me_x + 1))
        down_x = pltpu.make_async_remote_copy(
            src_ref=field.at[:, 1], dst_ref=field.at[:, nx + 1], send_sem=face_send.at[phase, 1],
            recv_sem=face_recv.at[phase, 1], device_id=at_x(me_x - 1))
        return up_x, down_x

    def copies_y(phase, half):
        up_y = pltpu.make_async_remote_copy(
            src_ref=packed.at[phase, half, 1], dst_ref=landed.at[phase, half, 0], device_id=at_y(me_y + 1),
            send_sem=face_send.at[phase, 2 + 2 * half], recv_sem=face_recv.at[phase, 2 + 2 * half])
        down_y = pltpu.make_async_remote_copy(
            src_ref=packed.at[phase, half, 0], dst_ref=landed.at[phase, half, 1], device_id=at_y(me_y - 1),
            send_sem=face_send.at[phase, 3 + 2 * half], recv_sem=face_recv.at[phase, 3 + 2 * half])
        return up_y, down_y

    def send(up, down, index, count):
        @pl.when(index < count - 1)
        def _():
            up.start()

        @pl.when(index > 0)
        def _():
            down.start()

    def receive(up, down, index, count):
        @pl.when(index > 0)
        def _():
            up.wait_recv()

        @pl.when(index < count - 1)
        def _():
            down.wait_recv()

    def finish(up, down, index, count):
        @pl.when(index < count - 1)
        def _():
            up.wait_send()

        @pl.when(index > 0)
        def _():
            down.wait_send()

    for field in (first, second):
        @pl.when(me_x == 0)
        def _():
            field[:, 0] = jnp.zeros((nz, cols, LANES), F32)

        @pl.when(me_x == n_gx - 1)
        def _():
            field[:, nx + 1] = jnp.zeros((nz, cols, LANES), F32)

    for phase in range(2):
        for half in range(2):
            @pl.when(me_y == 0)
            def _():
                landed[phase, half, 0] = jnp.zeros((cols, LANES), F32)

            @pl.when(me_y == n_gy - 1)
            def _():
                landed[phase, half, 1] = jnp.zeros((cols, LANES), F32)

    zero = jnp.zeros((cols, LANES), F32)
    middle = nx // 2
    faces = [copies(first, 0), copies(second, 1)]
    sides = [[copies_y(phase, half) for half in range(2)] for phase in range(2)]

    def edges(step, state):
        return lax.fori_loop(0, 2, lambda i, s: step(i * (nx - 1), s), state)

    def send_side(phase, half, state):
        packed[phase, half, 0], packed[phase, half, 1] = state
        send(*sides[phase][half], me_y, n_gy)

    load_x.wait()
    state = edges(take, (zero, zero))
    pl.semaphore_wait(barrier, n_gx + n_gy - 2)
    send(*faces[0], me_x, n_gx)
    send_side(0, 0, lax.fori_loop(1, middle, take, (zero, zero)))
    send_side(0, 1, lax.fori_loop(middle, nx - 1, take, state))
    load_kappa.wait()

    def apply_plane(field, phase, half, x):
        from_low, from_high = landed[phase, half, 0], landed[phase, half, 1]
        results = []
        for z in range(nz):
            g = z * nx + x
            center = field[z, x + 1]
            halo = jnp.where(lane == lax.rem(g + LANES - 1, LANES), from_low, from_high)
            halo = pltpu.roll(halo, lax.rem(LANES - g, LANES), 1)
            below = pltpu.roll(jnp.where(lane == LANES - 1, halo, center), 1, 1)
            above = pltpu.roll(jnp.where(lane == 0, halo, center), LANES - 1, 1)
            neighbours = field[z, x] + field[z, x + 2]
            neighbours = neighbours + (below + above)
            if z > 0:
                neighbours = neighbours + field[z - 1, x + 1]
            if z < nz - 1:
                neighbours = neighbours + field[z + 1, x + 1]
            coefficient = 6.0 + kappa_ref[pl.ds(g, 1), :]
            results.append(coefficient * center - neighbours)
        return results

    def first_plane(half, x, state):
        values = apply_plane(first, 0, half, x)
        for z in range(nz):
            second[z, x + 1] = values[z]
        return pack(x, values, state)

    receive(*sides[0][0], me_y, n_gy)
    state = lax.fori_loop(1, middle, functools.partial(first_plane, 0), (zero, zero))
    send_side(1, 0, state)
    receive(*sides[0][1], me_y, n_gy)
    receive(*faces[0], me_x, n_gx)
    state = edges(functools.partial(first_plane, 1), (zero, zero))
    send(*faces[1], me_x, n_gx)
    send_side(1, 1, lax.fori_loop(middle, nx - 1, functools.partial(first_plane, 1), state))

    def square(block):
        return lax.dot_general(block, block, (((1,), (1,)), ((), ())), preferred_element_type=F32)

    def second_plane(half, x, gram):
        values = jnp.concatenate(apply_plane(second, 1, half, x), axis=1)
        block = jnp.concatenate(split(values, 3), axis=0)
        parts[x] = block
        return gram + square(block)

    receive(*sides[1][0], me_y, n_gy)
    gram = jnp.zeros((3 * cols, 3 * cols), F32)
    gram = lax.fori_loop(1, middle, functools.partial(second_plane, 0), gram, unroll=True)
    receive(*sides[1][1], me_y, n_gy)
    gram = lax.fori_loop(middle, nx - 1, functools.partial(second_plane, 1), gram, unroll=True)
    receive(*faces[1], me_x, n_gx)
    gram = edges(functools.partial(second_plane, 1), gram)

    def fold(gram, terms):
        rows = fold_rows(gram, cols, terms)
        total = rows[:, :cols]
        for i in range(1, terms):
            total = total + rows[:, i * cols:(i + 1) * cols]
        return total

    def gather_copy(slots, stage, k, slot, axis_at, me, count, send_sem, recv_sem):
        return pltpu.make_async_remote_copy(
            src_ref=slots.at[stage, slot], dst_ref=slots.at[stage, slot], send_sem=send_sem.at[stage, k],
            recv_sem=recv_sem.at[stage, slot], device_id=axis_at(lax.rem(me + k, count)))

    def exchange(slots, stage, value, axis_at, me, count, send_sem, recv_sem):
        slots[stage, me] = value

        def copy(k, slot):
            return gather_copy(slots, stage, k, slot, axis_at, me, count, send_sem, recv_sem)

        @pl.loop(1, count)
        def _(k):
            copy(k, me).start()

        @pl.loop(1, count)
        def _(k):
            copy(k, lax.rem(me + k, count)).wait_recv()

        total = slots[stage, 0]
        for i in range(1, count):
            total = total + slots[stage, i]

        return total

    def reduced(gram, stage):
        per = LANES // cols
        height = cols // per
        dense = jnp.concatenate([gram[i * height:(i + 1) * height] for i in range(per)], axis=1)
        dense = exchange(gather_x, stage, dense, at_x, me_x, n_gx, gx_send, gx_recv)
        dense = exchange(gather_y, stage, dense, at_y, me_y, n_gy, gy_send, gy_recv)
        return jnp.concatenate([dense[:, i * cols:(i + 1) * cols] for i in range(per)], axis=0)

    def rows(stack, order):
        return jnp.concatenate([stack[i * cols:(i + 1) * cols] for i in order], axis=0)

    def columns(matrix, terms, order):
        pieces = split(matrix, terms)
        return jnp.concatenate([pieces[i] for i in order], axis=1)

    inverse = columns(inverse_factor(reduced(fold(gram, 3), 0), cols), 3, (0, 0, 0, 1, 1, 2))

    def solve_plane(x, gram):
        product = jnp.dot(inverse, rows(parts[x], (0, 1, 2, 0, 1, 0)), preferred_element_type=F32)
        block = jnp.concatenate(split(product, 2), axis=0)
        halves[x] = block
        pltpu.make_async_copy(halves.at[x], halves_hbm.at[x], store_sem.at[x]).start()
        return gram + square(block)

    gram = lax.fori_loop(0, nx, solve_plane, jnp.zeros((2 * cols, 2 * cols), F32), unroll=4)
    scale = math.sqrt(n_gx * n_gy * groups * LANES)
    again_ref[...] = columns(inverse_factor(reduced(fold(gram, 2), 1), cols) * scale, 2, (0, 0, 1, 1))

    @pl.loop(0, nx)
    def _(x):
        pltpu.make_async_copy(halves.at[x], halves_hbm.at[x], store_sem.at[x]).wait()

    for phase in range(2):
        finish(*faces[phase], me_x, n_gx)
        for half in range(2):
            finish(*sides[phase][half], me_y, n_gy)
        for slots, axis_at, me, count, send_sem, recv_sem in (
                (gather_x, at_x, me_x, n_gx, gx_send, gx_recv), (gather_y, at_y, me_y, n_gy, gy_send, gy_recv)):
            @pl.loop(1, count)
            def _(k):
                gather_copy(slots, phase, k, me, axis_at, me, count, send_sem, recv_sem).wait_send()


def finish_kernel(again_ref, halves_ref, o_ref):
    cols, deep, nx, ny = o_ref.shape
    flat = o_ref.reshape(cols * deep * nx, ny)

    def plane(x, carry):
        block = halves_ref[x]
        value = jnp.dot(again_ref[...], jnp.concatenate([block, block], axis=0), preferred_element_type=F32)
        for z in range(deep):
            flat[pl.ds(z * nx + x, cols, stride=deep * nx), :] = value[:, z * ny:(z + 1) * ny]
        return carry

    lax.fori_loop(0, nx, plane, 0, unroll=8)


def solution(mesh):
    n_gx, n_gy = mesh.shape["gx"], mesh.shape["gy"]

    def body(test_block, kappa_sq):
        cols, nz, nx, ny = test_block.shape
        dma = pltpu.SemaphoreType.DMA
        vmem = pl.BlockSpec(memory_space=pltpu.VMEM)
        height = cols * cols // LANES
        halves, again = pl.pallas_call(
            functools.partial(kernel, (n_gx, n_gy, cols, nz, nx)),
            out_shape=(jax.ShapeDtypeStruct((nx, 2 * cols, nz * ny), BF16),
                       jax.ShapeDtypeStruct((cols, 4 * cols), BF16)),
            in_specs=[pl.BlockSpec(memory_space=pltpu.HBM)] * 2,
            out_specs=(pl.BlockSpec(memory_space=pltpu.HBM), vmem),
            scratch_shapes=[
                pltpu.VMEM((cols * nz * nx, ny), F32),
                pltpu.VMEM((nz * nx, ny), F32),
                dma((2,)), dma((nx,)),
                pltpu.VMEM((nz, nx + 2, cols, ny), F32),
                pltpu.VMEM((nz, nx + 2, cols, ny), F32),
                pltpu.VMEM((nx, 3 * cols, nz * ny), BF16),
                pltpu.VMEM((nx, 2 * cols, nz * ny), BF16),
                pltpu.VMEM((2, 2, 2, cols, ny), F32),
                pltpu.VMEM((2, 2, 2, cols, ny), F32),
                pltpu.VMEM((2, n_gx, height, LANES), F32),
                pltpu.VMEM((2, n_gy, height, LANES), F32),
                dma((2, 6)), dma((2, 6)),
                dma((2, n_gx)), dma((2, n_gx)),
                dma((2, n_gy)), dma((2, n_gy)),
            ],
            compiler_params=pltpu.CompilerParams(
                collective_id=0, has_side_effects=True, vmem_limit_bytes=62 * 1024 * 1024),
        )(test_block.reshape(cols * nz * nx, ny), kappa_sq.reshape(nz * nx, ny))
        wide = 8
        return pl.pallas_call(
            finish_kernel,
            out_shape=jax.ShapeDtypeStruct(test_block.shape, F32),
            grid=(nx // wide,),
            in_specs=[vmem, pl.BlockSpec((wide, 2 * cols, nz * ny), lambda i: (i, 0, 0))],
            out_specs=pl.BlockSpec((cols, nz, wide, ny), lambda i: (0, 0, i, 0)),
            compiler_params=pltpu.CompilerParams(vmem_limit_bytes=62 * 1024 * 1024),
        )(again, halves)

    in_specs = (P(None, None, "gx", "gy"), P(None, "gx", "gy"))
    out_specs = P(None, None, "gx", "gy")
    return jax.shard_map(body, mesh=mesh, in_specs=in_specs, out_specs=out_specs, check_vma=False)
```
